32 devices in a mesh: groups: 2 (over x), dp: 16 (over z, y, core).
Axes of the slice: x: 2, y: 2, z: 4, core: 2. Of those that a mesh axis runs over, the one named last changes fastest.
Arguments:
- tokens: bfloat16 [1024, 5120], P(('groups', 'dp')), parts along dimension 0, may hold values from -6 to 6
- cotangent: bfloat16 [1024, 5120], P(('groups', 'dp')), parts along dimension 0, may hold values from -6 to 6
- w_gate: bfloat16 [5120, 24576], P(None, 'dp'), may hold values from -0.078125 to 0.078125
- w_up: bfloat16 [5120, 24576], P(None, 'dp'), may hold values from -0.078125 to 0.078125
- w_down: bfloat16 [24576, 5120], P('dp'), may hold values from -0.0390625 to 0.0390625
- model_factor: bfloat16 [5120, 128], replicated, may hold values from -0.078125 to 0.078125
- hidden_factor: bfloat16 [24576, 192], P('dp'), may hold values from -0.0390625 to 0.0390625
- lengths: int32 [32], P('groups'), parts along dimension 0, may hold values from 1 to 128, 512 in all
Outputs:
- grads: float32 [32, 12288], P(('groups', 'dp')), parts along dimension 0
The draws below stay inside these ranges and needn't reach their ends.
There are 2 independent parts, one for each index of `groups`. The reference program is written for one: setup_inputs(seed, part) draws one part's arguments, and reference() takes and returns one part's arrays. A program takes and returns all parts, laid end to end along the dimension named above; an argument that names none is the same for every part. Nothing has to cross between parts.
Inputs may be any that keep to these rules, and one draw needn't show every extreme that they name: The sequences' lengths in packing order; they sum to 512.
All inputs are finite; a program needn't handle non-finite values.
Results may differ from the reference program's by a relative error of at most 0.0029.
Values may be sent and summed in bfloat16 or wider, within the bound.
A program may use at most 128 MiB of HBM per device.

```python
import math
import jax
import jax.numpy as jnp
import numpy as np
from jax import lax

D = 5120
FF = 24576
RANK = 64
TOKENS = 512
SEQS = 16
LMAX = 128


def shard_levels(key, dims, pieces, smallest, high):
    def one(dim, shards_of):
        draws = jax.random.uniform(jax.random.fold_in(jax.random.fold_in(key, 6), dim), (shards_of,), jnp.float32, smallest / len(pieces), high / len(pieces))
        return jnp.repeat(jnp.exp(draws), dims[dim] // shards_of).reshape((-1,) + (1,) * (len(dims) - dim - 1))

    factor_of = one(*pieces[0])
    for cut in pieces[1:]:
        factor_of = factor_of * one(*cut)
    return factor_of


def split_up(number_of, total, limit, skew):
    loads = [(1 << 20) // math.isqrt(standing ** skew) + 1 for standing in range(2, number_of + 1)]
    surplus, holding = total - limit - (number_of - 1), [1] * (number_of - 1)
    while surplus > 0:
        movable = [i for i in range(number_of - 1) if holding[i] < limit]
        mass, budget = sum([loads[i] for i in movable]), surplus
        for i in movable:
            more = min(limit - holding[i], max(1, budget * loads[i] // mass), surplus)
            holding[i] = holding[i] + more
            surplus = surplus - more
    return np.array([limit] + holding)


def ragged_sizes(stream_key, count, total, reach, skew):
    if count == 2:
        one = jax.random.randint(stream_key, (), max(1, total - reach), min(reach, total - 1) + 1)
        return jnp.stack([one, total - one])
    sizes = jnp.asarray(split_up(count, total, reach, skew), jnp.int32)
    twos = (count - 1) // 2
    donor, taker = sizes[1:1 + 2 * twos:2], sizes[2:2 + 2 * twos:2]
    slack = jnp.minimum(donor - 1, reach - taker)
    shifted = jax.random.randint(jax.random.fold_in(stream_key, 1), (twos,), 0, 1 << 20) % (slack + 1)
    sizes = sizes.at[1:1 + 2 * twos:2].set(donor - shifted).at[2:2 + 2 * twos:2].set(taker + shifted)
    return sizes[jax.random.permutation(jax.random.fold_in(stream_key, 2), count)]


def normal_values(stream_key, shape, scale, limit, shards=(), kind=jnp.bfloat16):
    values = scale * jax.random.normal(stream_key, shape, jnp.float32)
    if shards:
        values = values * shard_levels(stream_key, shape, shards, -0.22, 0.18)
    return jnp.clip(values, -limit, limit).astype(kind)


def setup_inputs(seed: int = 0, part: int = 0) -> dict:
    keys = jax.random.split(jax.random.key(seed), 9)
    part_keys = jax.random.split(jax.random.fold_in(keys[8], part), 9)
    tokens = normal_values(part_keys[0], (TOKENS, D), 1.0, 6.0, ((0, 16),))
    cotangent = normal_values(part_keys[1], (TOKENS, D), 1.0, 6.0, ((0, 16),))
    w_gate = normal_values(keys[2], (D, FF), D ** -0.5, 0.078125, ((1, 16),))
    w_up = normal_values(keys[3], (D, FF), D ** -0.5, 0.078125, ((1, 16),))
    w_down = normal_values(keys[4], (FF, D), FF ** -0.5, 0.0390625, ((0, 16),))
    model_factor = normal_values(keys[5], (D, 2 * RANK), D ** -0.5, 0.078125)
    hidden_factor = normal_values(keys[6], (FF, 3 * RANK), FF ** -0.5, 0.0390625, ((0, 16),))
    lengths = ragged_sizes(part_keys[7], SEQS, TOKENS, LMAX, 2).astype(jnp.int32)
    return dict(tokens=tokens, cotangent=cotangent, w_gate=w_gate, w_up=w_up, w_down=w_down, model_factor=model_factor, hidden_factor=hidden_factor, lengths=lengths)


def outer_sums(onehot, left, right, count, rank):
    spread = (onehot[:, :, None] * left[:, None, :]).reshape(left.shape[0], count * rank)
    total = jnp.dot(spread.T, right, precision=lax.Precision.HIGHEST, preferred_element_type=jnp.float32)
    return total.reshape(count, rank * rank)


def reference(tokens, cotangent, w_gate, w_up, w_down, model_factor, hidden_factor, lengths):
    rank = model_factor.shape[1] // 2
    gate = jnp.dot(tokens, w_gate, preferred_element_type=jnp.float32)
    up = jnp.dot(tokens, w_up, preferred_element_type=jnp.float32)
    sig = jax.nn.sigmoid(gate)
    hidden = (gate * sig * up).astype(jnp.bfloat16)
    back = jnp.dot(cotangent, w_down.T, preferred_element_type=jnp.float32)
    d_up = (back * gate * sig).astype(jnp.bfloat16)
    d_gate = (back * up * sig * (1.0 + gate * (1.0 - sig))).astype(jnp.bfloat16)
    feat_gate = jnp.dot(d_gate, hidden_factor[:, 0:rank], preferred_element_type=jnp.float32)
    feat_up = jnp.dot(d_up, hidden_factor[:, rank:2 * rank], preferred_element_type=jnp.float32)
    feat_hidden = jnp.dot(hidden, hidden_factor[:, 2 * rank:3 * rank], preferred_element_type=jnp.float32)
    feat_in = jnp.dot(tokens, model_factor[:, 0:rank], preferred_element_type=jnp.float32)
    feat_out = jnp.dot(cotangent, model_factor[:, rank:2 * rank], preferred_element_type=jnp.float32)
    ends = jnp.cumsum(lengths).astype(jnp.int32)
    positions = jnp.arange(tokens.shape[0], dtype=jnp.int32)
    seg = jnp.sum((positions[:, None] >= ends[None, :]).astype(jnp.int32), axis=1).astype(jnp.int32)
    count = lengths.shape[0]
    onehot = (seg[:, None] == jnp.arange(count, dtype=jnp.int32)[None, :]).astype(jnp.float32)
    first = outer_sums(onehot, feat_in, feat_gate, count, rank)
    second = outer_sums(onehot, feat_in, feat_up, count, rank)
    third = outer_sums(onehot, feat_hidden, feat_out, count, rank)
    return jnp.concatenate([first, second, third], axis=1)
```

```python
import functools

import jax
import jax.numpy as jnp
from jax import lax
from jax.experimental import pallas as pl
from jax.experimental.pallas import tpu as pltpu
from jax.sharding import PartitionSpec as P

MESH = pl.DeviceIdType.MESH
PIECES = 10
WSLOTS = 3
WIRE = jnp.bfloat16


def when(cond, fn):
    pl.when(cond)(fn)


def both(a, b):
    return jnp.logical_and(a, b)


def kernel(
    Z, Y, lengths, tokens, cot, w_gate, w_up, w_down, mf_hbm, hf_hbm, out,
    buf, acc_g, acc_u, acc_b, acc_m, feats, wg, wu, wd, mf, hf,
    part, r1, s2, r2, r3, s3,
    recv_sem, send_sem, own_sem, wsem, dsem, fsem, rs_send, rs_recv, z_send, z_recv,
):
    n, C = PIECES, wg.shape[1]
    K = 2 * n
    rows_dev = tokens.shape[0]
    N = Z * Y * 2
    T = N * rows_dev
    FFD = w_gate.shape[1]
    S = lengths.shape[0]
    me = lax.axis_index("dp")
    c = lax.rem(me, 2)
    y = lax.rem(me // 2, Y)
    z = me // (2 * Y)

    def index(zz, yy, cc):
        return (zz * Y + yy) * 2 + cc

    sib = index(z, y, 1 - c)
    ynb = index(z, Y - 1 - y, c)

    def column():
        for step in range(1, Z):
            yield step, lax.rem(z + step, Z)

    def own_copy(k_static):
        src = tokens if k_static < n else cot
        col = (k_static % n) * C
        return pltpu.make_async_copy(
            src.at[:, pl.ds(col, C)], buf.at[k_static, me], own_sem.at[k_static]
        )

    for k in range(K):
        own_copy(k).start()

    def weight_copies(k, slot):
        rows = pl.ds(pl.multiple_of(k * C, C), C)
        return (
            pltpu.make_async_copy(w_gate.at[rows, :], wg.at[slot], wsem.at[slot, 0]),
            pltpu.make_async_copy(w_up.at[rows, :], wu.at[slot], wsem.at[slot, 1]),
        )

    def down_copy(k, slot):
        cols = pl.ds(pl.multiple_of(k * C, C), C)
        return pltpu.make_async_copy(w_down.at[:, cols], wd.at[slot], dsem.at[slot])

    mf_copy = pltpu.make_async_copy(mf_hbm, mf, fsem.at[0])
    hf_copy = pltpu.make_async_copy(hf_hbm, hf, fsem.at[1])
    mf_copy.start()
    for j in range(WSLOTS):
        for cp in weight_copies(j, j):
            cp.start()
    hf_copy.start()
    for j in range(WSLOTS):
        down_copy(j, j).start()

    barrier = pltpu.get_barrier_semaphore()
    partners = [sib] + ([ynb] if Y > 1 else []) + [index(zz, y, c) for _, zz in column()]
    for p in partners:
        pl.semaphore_signal(barrier, inc=1, device_id={"dp": p}, device_id_type=MESH)
    pl.semaphore_wait(barrier, len(partners))

    def block(k, o, slot, dest):
        return pltpu.make_async_remote_copy(
            src_ref=buf.at[k, o],
            dst_ref=buf.at[k, o],
            send_sem=send_sem.at[k, slot],
            recv_sem=recv_sem.at[k, o],
            device_id={"dp": dest},
            device_id_type=MESH,
        )

    def wait_block(k, o):
        block(k, o, 0, sib).wait_recv()

    def send_down(k, zz):
        return block(k, index(zz, y, c), zz, index(z - 1, y, c))

    def send_up(k, zz):
        return block(k, index(zz, y, c), zz, index(z + 1, y, c))

    def send_y(k, zz):
        return block(k, index(zz, y, c), Z + zz, ynb)

    def send_sib(k, zz, yy):
        return block(k, index(zz, yy, c), 2 * Z + zz * Y + yy, sib)

    def own_sends(k):
        yield z < Z - 1, lambda: block(k, me, 2 * Z + Z * Y, index(z + 1, y, c))
        yield z > 0, lambda: block(k, me, 2 * Z + Z * Y + 1, index(z - 1, y, c))
        if Y > 1:
            yield None, lambda: send_y(k, z)
        yield None, lambda: send_sib(k, z, y)

    def relay_sends(k, r, above):
        zz = z + r if above else z - r
        if above:
            yield z > 0, lambda: send_down(k, zz)
        else:
            yield z < Z - 1, lambda: send_up(k, zz)
        if Y > 1:
            yield None, lambda: send_y(k, zz)
        yield None, lambda: send_sib(k, zz, y)

    def run(sends, act):
        for cond, make in sends:
            if cond is None:
                act(make())
            else:
                when(cond, functools.partial(lambda m: act(m()), make))

    start = lambda cp: cp.start()
    done = lambda cp: cp.wait_send()

    def here(r, above):
        return (z + r < Z) if above else (z - r >= 0)

    def own_stage(k):
        pltpu.make_async_copy(
            tokens.at[:, pl.ds(0, C)], buf.at[k, me], own_sem.at[k]
        ).wait()
        run(own_sends(k), start)

    def relay_stage(k, r):
        for above in (True, False):
            def arrived(above=above):
                zz = z + r if above else z - r
                wait_block(k, index(zz, y, c))
                run(relay_sends(k, r, above), start)
            when(here(r, above), arrived)

    def y_stage(k, r):
        for above in (True, False) if r else (True,):
            def arrived(above=above):
                zz = z + r if above else z - r
                wait_block(k, index(zz, Y - 1 - y, c))
                send_sib(k, zz, Y - 1 - y).start()
            when(here(r, above), arrived)

    def sib_stage(k):
        for zz in range(Z):
            for yy in range(Y):
                wait_block(k, index(zz, yy, 1 - c))

    acc_g[...] = jnp.zeros_like(acc_g)
    acc_u[...] = jnp.zeros_like(acc_u)
    acc_b[...] = jnp.zeros_like(acc_b)
    acc_m[...] = jnp.zeros_like(acc_m)
    mf_copy.wait()
    hf_copy.wait()
    lane = lax.broadcasted_iota(jnp.int32, (T, 128), 1)
    TILE = 256 if FFD % 256 == 0 else FFD
    RB = T // 8

    def compute(k):
        lhs = buf[k].reshape(T, C)
        kk = lax.rem(k, n)
        slot = lax.rem(kk, WSLOTS)
        mrows = pl.ds(pl.multiple_of(kk * C, C), C)
        mod = jnp.dot(lhs, mf[mrows, :], preferred_element_type=jnp.float32)
        first = k < n
        acc_m[...] += jnp.where((lane < 64) == first, mod, 0.0)

        def forward():
            for cp in weight_copies(kk, slot):
                cp.wait()

            def tile(j, carry):
                cols = pl.ds(pl.multiple_of(j * TILE, TILE), TILE)
                acc_g[:, cols] += jnp.dot(
                    lhs, wg[slot, :, cols], preferred_element_type=jnp.float32
                )
                acc_u[:, cols] += jnp.dot(
                    lhs, wu[slot, :, cols], preferred_element_type=jnp.float32
                )
                return carry

            lax.fori_loop(0, FFD // TILE, tile, 0)

            def more():
                for cp in weight_copies(kk + WSLOTS, slot):
                    cp.start()

            when(kk + WSLOTS < n, more)

        def backward():
            down_copy(kk, slot).wait()

            def tile(j, carry):
                cols = pl.ds(pl.multiple_of(j * TILE, TILE), TILE)
                acc_b[:, cols] += lax.dot_general(
                    lhs, wd[slot, cols, :], (((1,), (1,)), ((), ())),
                    preferred_element_type=jnp.float32,
                )
                return carry

            lax.fori_loop(0, FFD // TILE, tile, 0)
            when(kk + WSLOTS < n, lambda: down_copy(kk + WSLOTS, slot).start())

            def gating():
                rows = pl.ds(pl.multiple_of(kk * RB, RB), RB)
                gate = acc_g[rows, :]
                up = acc_u[rows, :]
                sig = jax.nn.sigmoid(gate)
                gs = gate * sig
                hidden = (gs * up).astype(jnp.bfloat16)
                acc_g[rows, :] = gs
                acc_u[rows, :] = up * sig * (1.0 + gate * (1.0 - sig))
                fh = jnp.dot(hidden, hf[...], preferred_element_type=jnp.float32)
                feats[rows, 128:192] = fh[:, 128:192]

            when(kk < 8, gating)

        when(first, forward)
        when(jnp.logical_not(first), backward)

    LAG = Z + 1
    AHEAD = 1

    for k in range(AHEAD):
        own_stage(k)

    def step(t, carry):
        when(t + AHEAD < K, lambda: own_stage(t + AHEAD))
        for r in range(1, Z):
            when(both(t >= r, t - r < K), functools.partial(relay_stage, t - r, r))
        if Y > 1:
            for r in range(Z):
                when(both(t >= r + 1, t - r - 1 < K), functools.partial(y_stage, t - r - 1, r))
        def ready():
            sib_stage(t - LAG)
            compute(t - LAG)
        when(t >= LAG, ready)
        return carry

    lax.fori_loop(0, K + LAG, step, 0)

    FB = 128

    def finish(i, carry):
        rows = pl.ds(pl.multiple_of(i * FB, FB), FB)
        back = acc_b[rows, :]
        d_gate = (back * acc_u[rows, :]).astype(jnp.bfloat16)
        d_up = (back * acc_g[rows, :]).astype(jnp.bfloat16)
        fg = jnp.dot(d_gate, hf[...], preferred_element_type=jnp.float32)
        fu = jnp.dot(d_up, hf[...], preferred_element_type=jnp.float32)
        feats[rows, 0:128] = jnp.where(lane[:FB] < 64, fg[:, 0:128], fu[:, 0:128])
        return carry

    lax.fori_loop(0, T // FB, finish, 0)

    right = feats[...]
    right_hi = right.astype(jnp.bfloat16)
    right_lo = (right - right_hi.astype(jnp.float32)).astype(jnp.bfloat16)
    left = acc_m[...].T
    pos = lax.broadcasted_iota(jnp.int32, (128, T), 1)
    begin = jnp.int32(0)
    G = 4
    for s0 in range(0, S, G):
        his, los = [], []
        for s in range(s0, s0 + G):
            end = begin + lengths[s]
            picked = jnp.where(both(pos >= begin, pos < end), left, 0.0)
            hi = picked.astype(jnp.bfloat16)
            his.append(hi)
            los.append((picked - hi.astype(jnp.float32)).astype(jnp.bfloat16))
            begin = end
        hi = jnp.concatenate(his, axis=0)
        lo = jnp.concatenate(los, axis=0)
        sums = (
            jnp.dot(hi, right_hi, preferred_element_type=jnp.float32)
            + jnp.dot(hi, right_lo, preferred_element_type=jnp.float32)
            + jnp.dot(lo, right_hi, preferred_element_type=jnp.float32)
        )
        for s in range(s0, s0 + G):
            one = sums[(s - s0) * 128 : (s - s0 + 1) * 128]
            cc, yy, zz = s % 2, (s // 2) % Y, s // (2 * Y)
            part[cc, yy, zz, 0:64, :] = one[0:64, 0:128]
            part[cc, yy, zz, 64:96, :] = jnp.concatenate(
                [one[64:96, 128:192], one[96:128, 128:192]], axis=1
            )

    core_send = pltpu.make_async_remote_copy(
        src_ref=part.at[1 - c], dst_ref=r1, send_sem=rs_send.at[0], recv_sem=rs_recv.at[0],
        device_id={"dp": sib}, device_id_type=MESH,
    )
    core_send.start()
    core_send.wait_recv()
    if Y > 1:
        s2[...] = (part[c, 1 - y] + r1[1 - y]).astype(WIRE)
        y_send = pltpu.make_async_remote_copy(
            src_ref=s2, dst_ref=r2, send_sem=rs_send.at[1], recv_sem=rs_recv.at[1],
            device_id={"dp": ynb}, device_id_type=MESH,
        )
        y_send.start()
        y_send.wait_recv()

    def total(zz):
        value = part[c, y, zz] + r1[y, zz]
        if Y > 1:
            value = value + r2[zz].astype(jnp.float32)
        return value

    sends = []
    for step_z, zz in column():
        s3[step_z] = total(zz).astype(WIRE)
        cp = pltpu.make_async_remote_copy(
            src_ref=s3.at[step_z], dst_ref=r3.at[step_z], send_sem=z_send.at[step_z],
            recv_sem=z_recv.at[step_z], device_id={"dp": index(zz, y, c)}, device_id_type=MESH,
        )
        cp.start()
        sends.append(cp)
    value = total(z)
    for i, cp in enumerate(sends):
        cp.wait_recv()
        value = value + r3[i + 1].astype(jnp.float32)
    out[...] = value

    core_send.wait_send()
    if Y > 1:
        y_send.wait_send()
    for cp in sends:
        cp.wait_send()

    def drain(k, carry):
        run(own_sends(k), done)
        for r in range(1, Z):
            for above in (True, False):
                when(here(r, above), functools.partial(run, list(relay_sends(k, r, above)), done))
        if Y > 1:
            for r in range(Z):
                for above in (True, False) if r else (True,):
                    zz = z + r if above else z - r
                    when(
                        here(r, above),
                        functools.partial(lambda q: send_sib(k, q, Y - 1 - y).wait_send(), zz),
                    )
        return carry

    lax.fori_loop(0, K, drain, 0)


def body(Z, Y, tokens, cotangent, w_gate, w_up, w_down, model_factor, hidden_factor, lengths):
    rows, D = tokens.shape
    FFD = w_gate.shape[1]
    N = Z * Y * 2
    T = N * rows
    n = PIECES
    C = D // n
    K = 2 * n
    f32, bf16 = jnp.float32, jnp.bfloat16
    any_spec = pl.BlockSpec(memory_space=pl.ANY)
    dma = pltpu.SemaphoreType.DMA
    out = pl.pallas_call(
        functools.partial(kernel, Z, Y),
        out_shape=jax.ShapeDtypeStruct((96, 128), f32),
        in_specs=[pl.BlockSpec(memory_space=pltpu.SMEM)] + [any_spec] * 7,
        out_specs=pl.BlockSpec(memory_space=pltpu.VMEM),
        scratch_shapes=[
            pltpu.VMEM((K, N, rows, C), bf16),
            pltpu.VMEM((T, FFD), f32),
            pltpu.VMEM((T, FFD), f32),
            pltpu.VMEM((T, FFD), f32),
            pltpu.VMEM((T, 128), f32),
            pltpu.VMEM((T, 192), f32),
            pltpu.VMEM((WSLOTS, C, FFD), bf16),
            pltpu.VMEM((WSLOTS, C, FFD), bf16),
            pltpu.VMEM((WSLOTS, FFD, C), bf16),
            pltpu.VMEM(model_factor.shape, bf16),
            pltpu.VMEM(hidden_factor.shape, bf16),
            pltpu.VMEM((2, Y, Z, 96, 128), f32),
            pltpu.VMEM((Y, Z, 96, 128), f32),
            pltpu.VMEM((Z, 96, 128), WIRE),
            pltpu.VMEM((Z, 96, 128), WIRE),
            pltpu.VMEM((Z, 96, 128), WIRE),
            pltpu.VMEM((Z, 96, 128), WIRE),
            dma((K, N)),
            dma((K, 2 * Z + Z * Y + 2)),
            dma((K,)),
            dma((WSLOTS, 2)),
            dma((WSLOTS,)),
            dma((2,)),
            dma((2,)),
            dma((2,)),
            dma((Z,)),
            dma((Z,)),
        ],
        compiler_params=pltpu.CompilerParams(
            collective_id=0, has_side_effects=True, vmem_limit_bytes=60 * 1024 * 1024
        ),
        cost_estimate=pl.CostEstimate(
            flops=6 * T * D * FFD, bytes_accessed=6 * D * FFD, transcendentals=T * FFD
        ),
    )(lengths, tokens, cotangent, w_gate, w_up, w_down, model_factor, hidden_factor)
    first = out[0:64, 0:64].reshape(1, 4096)
    second = out[0:64, 64:128].reshape(1, 4096)
    third = jnp.concatenate([out[64:96, 0:64], out[64:96, 64:128]], axis=0).T.reshape(1, 4096)
    return jnp.concatenate([first, second, third], axis=1)


def solution(mesh):
    devices = mesh.shape["dp"]
    Y = 2 if mesh.shape["groups"] == 2 else 1
    placed = (
        P(("groups", "dp"), None),
        P(("groups", "dp"), None),
        P(None, "dp"),
        P(None, "dp"),
        P("dp", None),
        P(),
        P("dp", None),
        P("groups"),
    )
    return jax.shard_map(
        functools.partial(body, devices // (2 * Y), Y),
        mesh=mesh, in_specs=placed, out_specs=P(("groups", "dp"), None), check_vma=False,
    )
```

```python
import functools

import jax
import jax.numpy as jnp
from jax import lax
from jax.experimental import pallas as pl
from jax.experimental.pallas import tpu as pltpu
from jax.sharding import PartitionSpec as P

MESH = pl.DeviceIdType.MESH
PIECES = 5
WSLOTS = 2
Y_EVERY = 5
HOP = 1
AHEAD = 1
WIRE = jnp.bfloat16


def when(cond, fn):
    pl.when(cond)(fn)


def both(a, b):
    return jnp.logical_and(a, b)


def kernel(
    Z, Y, lengths, tokens, cot, w_gate, w_up, w_down, mf_hbm, hf_hbm, out,
    buf, acc_g, acc_u, acc_b, acc_m, feats, wg, wu, wd, mf, hf,
    part, r1, s2, r2, r3, s3,
    recv_sem, send_sem, own_sem, wsem, dsem, fsem, rs_send, rs_recv, z_send, z_recv,
):
    n, C = PIECES, wg.shape[1]
    K = 2 * n
    rows_dev = tokens.shape[0]
    N = Z * Y * 2
    T = N * rows_dev
    FFD = w_gate.shape[1]
    S = lengths.shape[0]
    me = lax.axis_index("dp")
    c = lax.rem(me, 2)
    y = lax.rem(me // 2, Y)
    z = me // (2 * Y)

    def index(zz, yy, cc):
        return (zz * Y + yy) * 2 + cc

    sib = index(z, y, 1 - c)
    ynb = index(z, Y - 1 - y, c)

    def column():
        for step in range(1, Z):
            yield step, lax.rem(z + step, Z)

    def own_copy(k_static):
        src = tokens if k_static < n else cot
        col = (k_static % n) * C
        return pltpu.make_async_copy(
            src.at[:, pl.ds(col, C)], buf.at[k_static, me], own_sem.at[k_static]
        )

    for k in range(K):
        own_copy(k).start()

    def weight_copies(k, slot):
        rows = pl.ds(pl.multiple_of(k * C, C), C)
        return (
            pltpu.make_async_copy(w_gate.at[rows, :], wg.at[slot], wsem.at[slot, 0]),
            pltpu.make_async_copy(w_up.at[rows, :], wu.at[slot], wsem.at[slot, 1]),
        )

    def down_copy(k, slot):
        cols = pl.ds(pl.multiple_of(k * C, C), C)
        return pltpu.make_async_copy(w_down.at[:, cols], wd.at[slot], dsem.at[slot])

    mf_copy = pltpu.make_async_copy(mf_hbm, mf, fsem.at[0])
    hf_copy = pltpu.make_async_copy(hf_hbm, hf, fsem.at[1])
    mf_copy.start()
    for j in range(WSLOTS):
        for cp in weight_copies(j, j):
            cp.start()
    hf_copy.start()
    for j in range(WSLOTS):
        down_copy(j, j).start()

    barrier = pltpu.get_barrier_semaphore()
    partners = [sib] + ([ynb] if Y > 1 else []) + [index(zz, y, c) for _, zz in column()]
    for p in partners:
        pl.semaphore_signal(barrier, inc=1, device_id={"dp": p}, device_id_type=MESH)
    pl.semaphore_wait(barrier, len(partners))

    def block(k, o, slot, dest):
        return pltpu.make_async_remote_copy(
            src_ref=buf.at[k, o],
            dst_ref=buf.at[k, o],
            send_sem=send_sem.at[k, slot],
            recv_sem=recv_sem.at[k, o],
            device_id={"dp": dest},
            device_id_type=MESH,
        )

    def wait_block(k, o):
        block(k, o, 0, sib).wait_recv()

    def y_first(k):
        return lax.rem(k, Y_EVERY) == Y_EVERY // 2

    def send_down(k, zz):
        return block(k, index(zz, y, c), zz, index(z - 1, y, c))

    def send_up(k, zz):
        return block(k, index(zz, y, c), zz, index(z + 1, y, c))

    def send_y(k, zz):
        return block(k, index(zz, y, c), Z + zz, ynb)

    def send_sib(k, zz, yy):
        return block(k, index(zz, yy, c), 2 * Z + zz * Y + yy, sib)

    def own_sends(k):
        yield z < Z - 1, lambda: block(k, me, 2 * Z + Z * Y, index(z + 1, y, c))
        yield z > 0, lambda: block(k, me, 2 * Z + Z * Y + 1, index(z - 1, y, c))
        if Y > 1:
            yield None, lambda: send_y(k, z)
        yield None, lambda: send_sib(k, z, y)

    def relay_sends(k, r, above):
        zz = z + r if above else z - r
        if above:
            yield z > 0, lambda: send_down(k, zz)
        else:
            yield z < Z - 1, lambda: send_up(k, zz)
        if Y > 1:
            yield jnp.logical_not(y_first(k)), lambda: send_y(k, zz)
        yield None, lambda: send_sib(k, zz, y)

    def other_sends(k, r, above):
        zz = z + r if above else z - r
        o = index(zz, Y - 1 - y, c)
        up, down = index(z + 1, y, c), index(z - 1, y, c)
        base = 2 * Z + Z * Y + 2
        if r == 0 or not above:
            yield both(y_first(k), z < Z - 1), lambda: block(k, o, base + zz, up)
        if r == 0:
            yield both(y_first(k), z > 0), lambda: block(k, o, base + Z, down)
        elif above:
            yield both(y_first(k), z > 0), lambda: block(k, o, base + zz, down)
        yield None, lambda: send_sib(k, zz, Y - 1 - y)

    def run(sends, act):
        for cond, make in sends:
            if cond is None:
                act(make())
            else:
                when(cond, functools.partial(lambda m: act(m()), make))

    start = lambda cp: cp.start()
    done = lambda cp: cp.wait_send()

    def here(r, above):
        return (z + r < Z) if above else (z - r >= 0)

    def own_stage(k):
        pltpu.make_async_copy(
            tokens.at[:, pl.ds(0, C)], buf.at[k, me], own_sem.at[k]
        ).wait()
        run(own_sends(k), start)

    def relay_stage(k, r):
        for above in (True, False):
            def arrived(above=above):
                zz = z + r if above else z - r
                wait_block(k, index(zz, y, c))
                run(relay_sends(k, r, above), start)
            when(here(r, above), arrived)

    def y_stage(k, r):
        for above in (True, False) if r else (True,):
            def arrived(above=above):
                zz = z + r if above else z - r
                wait_block(k, index(zz, Y - 1 - y, c))
                run(other_sends(k, r, above), start)
            when(here(r, above), arrived)

    def sib_stage(k):
        for zz in range(Z):
            for yy in range(Y):
                wait_block(k, index(zz, yy, 1 - c))

    for k in range(AHEAD):
        own_stage(k)

    acc_g[...] = jnp.zeros_like(acc_g)
    acc_u[...] = jnp.zeros_like(acc_u)
    acc_b[...] = jnp.zeros_like(acc_b)
    acc_m[...] = jnp.zeros_like(acc_m)
    mf_copy.wait()
    hf_copy.wait()
    lane = lax.broadcasted_iota(jnp.int32, (T, 128), 1)
    TILE = FFD // 2
    GATING = 8 if n >= 8 else 4
    RB = T // GATING

    def project(rows):
        return lax.dot_general(
            rows, hf[...], (((1,), (1,)), ((), ())), preferred_element_type=jnp.float32
        )

    def compute(k):
        lhs = buf[k].reshape(T, C)
        kk = lax.rem(k, n)
        slot = lax.rem(kk, WSLOTS)
        mrows = pl.ds(pl.multiple_of(kk * C, C), C)
        mod = jnp.dot(lhs, mf[mrows, :], preferred_element_type=jnp.float32)
        first = k < n
        acc_m[...] += jnp.where((lane < 64) == first, mod, 0.0)

        def forward():
            for cp in weight_copies(kk, slot):
                cp.wait()

            def tile(j, carry):
                cols = pl.ds(pl.multiple_of(j * TILE, TILE), TILE)
                acc_g[:, cols] += jnp.dot(
                    lhs, wg[slot, :, cols], preferred_element_type=jnp.float32
                )
                acc_u[:, cols] += jnp.dot(
                    lhs, wu[slot, :, cols], preferred_element_type=jnp.float32
                )
                return carry

            lax.fori_loop(0, FFD // TILE, tile, 0)

            def more():
                for cp in weight_copies(kk + WSLOTS, slot):
                    cp.start()

            when(kk + WSLOTS < n, more)

        def backward():
            down_copy(kk, slot).wait()

            def tile(j, carry):
                cols = pl.ds(pl.multiple_of(j * TILE, TILE), TILE)
                acc_b[:, cols] += lax.dot_general(
                    lhs, wd[slot, cols, :], (((1,), (1,)), ((), ())),
                    preferred_element_type=jnp.float32,
                )
                return carry

            lax.fori_loop(0, FFD // TILE, tile, 0)
            when(kk + WSLOTS < n, lambda: down_copy(kk + WSLOTS, slot).start())

            def gating():
                rows = pl.ds(pl.multiple_of(kk * RB, RB), RB)
                gate = acc_g[rows, :]
                up = acc_u[rows, :]
                sig = jax.nn.sigmoid(gate)
                gs = gate * sig
                hidden = (gs * up).astype(jnp.bfloat16)
                acc_g[rows, :] = gs
                acc_u[rows, :] = up * sig * (1.0 + gate * (1.0 - sig))
                fh = project(hidden)
                feats[rows, 128:192] = fh[:, 128:192]

            when(kk < GATING, gating)

        when(first, forward)
        when(jnp.logical_not(first), backward)

    LAG = HOP * (Z + 1)

    def step(t, carry):
        for r in range(1, Z):
            k = t - HOP * r + HOP - 1
            when(both(k >= 0, k < K), functools.partial(relay_stage, k, r))
        if Y > 1:
            for r in range(Z):
                k = t - HOP * (r + 1) + HOP - 1
                when(both(k >= 0, k < K), functools.partial(y_stage, k, r))

        when(t + AHEAD < K, lambda: own_stage(t + AHEAD))

        def ready():
            sib_stage(t - LAG)
            compute(t - LAG)

        when(t >= LAG, ready)
        return carry

    lax.fori_loop(0, K + LAG, step, 0)

    FB = 128

    def finish(i, carry):
        rows = pl.ds(pl.multiple_of(i * FB, FB), FB)
        back = acc_b[rows, :]
        d_gate = (back * acc_u[rows, :]).astype(jnp.bfloat16)
        d_up = (back * acc_g[rows, :]).astype(jnp.bfloat16)
        fg = project(d_gate)
        fu = project(d_up)
        feats[rows, 0:128] = jnp.where(lane[:FB] < 64, fg[:, 0:128], fu[:, 0:128])
        return carry

    lax.fori_loop(0, T // FB, finish, 0)

    right = feats[...]
    right_hi = right.astype(jnp.bfloat16)
    right_lo = (right - right_hi.astype(jnp.float32)).astype(jnp.bfloat16)
    left = acc_m[...].T
    pos = lax.broadcasted_iota(jnp.int32, (128, T), 1)
    begin = jnp.int32(0)
    G = 4
    for s0 in range(0, S, G):
        his, los = [], []
        for s in range(s0, s0 + G):
            end = begin + lengths[s]
            picked = jnp.where(both(pos >= begin, pos < end), left, 0.0)
            hi = picked.astype(jnp.bfloat16)
            his.append(hi)
            los.append((picked - hi.astype(jnp.float32)).astype(jnp.bfloat16))
            begin = end
        hi = jnp.concatenate(his, axis=0)
        lo = jnp.concatenate(los, axis=0)
        sums = (
            jnp.dot(hi, right_hi, preferred_element_type=jnp.float32)
            + jnp.dot(hi, right_lo, preferred_element_type=jnp.float32)
            + jnp.dot(lo, right_hi, preferred_element_type=jnp.float32)
        )
        for s in range(s0, s0 + G):
            one = sums[(s - s0) * 128 : (s - s0 + 1) * 128]
            cc, yy, zz = s % 2, (s // 2) % Y, s // (2 * Y)
            part[cc, yy, zz, 0:64, :] = one[0:64, 0:128]
            part[cc, yy, zz, 64:96, :] = jnp.concatenate(
                [one[64:96, 128:192], one[96:128, 128:192]], axis=1
            )

    def drain(k, carry):
        run(own_sends(k), done)
        for r in range(1, Z):
            for above in (True, False):
                when(here(r, above), functools.partial(run, list(relay_sends(k, r, above)), done))
        if Y > 1:
            for r in range(Z):
                for above in (True, False) if r else (True,):
                    when(here(r, above), functools.partial(run, list(other_sends(k, r, above)), done))
        return carry

    core_send = pltpu.make_async_remote_copy(
        src_ref=part.at[1 - c], dst_ref=r1, send_sem=rs_send.at[0], recv_sem=rs_recv.at[0],
        device_id={"dp": sib}, device_id_type=MESH,
    )
    core_send.start()
    lax.fori_loop(0, n, drain, 0)
    core_send.wait_recv()
    if Y > 1:
        s2[...] = (part[c, 1 - y] + r1[1 - y]).astype(WIRE)
        y_send = pltpu.make_async_remote_copy(
            src_ref=s2, dst_ref=r2, send_sem=rs_send.at[1], recv_sem=rs_recv.at[1],
            device_id={"dp": ynb}, device_id_type=MESH,
        )
        y_send.start()
        lax.fori_loop(n, K, drain, 0)
        y_send.wait_recv()
    else:
        lax.fori_loop(n, K, drain, 0)

    def total(zz):
        value = part[c, y, zz] + r1[y, zz]
        if Y > 1:
            value = value + r2[zz].astype(jnp.float32)
        return value

    sends = []
    for step_z, zz in column():
        s3[step_z] = total(zz).astype(WIRE)
        cp = pltpu.make_async_remote_copy(
            src_ref=s3.at[step_z], dst_ref=r3.at[step_z], send_sem=z_send.at[step_z],
            recv_sem=z_recv.at[step_z], device_id={"dp": index(zz, y, c)}, device_id_type=MESH,
        )
        cp.start()
        sends.append(cp)
    value = total(z)
    for i, cp in enumerate(sends):
        cp.wait_recv()
        value = value + r3[i + 1].astype(jnp.float32)
    out[...] = value

    core_send.wait_send()
    if Y > 1:
        y_send.wait_send()
    for cp in sends:
        cp.wait_send()


def body(Z, Y, tokens, cotangent, w_gate, w_up, w_down, model_factor, hidden_factor, lengths):
    rows, D = tokens.shape
    FFD = w_gate.shape[1]
    N = Z * Y * 2
    T = N * rows
    n = PIECES
    C = D // n
    K = 2 * n
    f32, bf16 = jnp.float32, jnp.bfloat16
    any_spec = pl.BlockSpec(memory_space=pl.ANY)
    dma = pltpu.SemaphoreType.DMA
    out = pl.pallas_call(
        functools.partial(kernel, Z, Y),
        out_shape=jax.ShapeDtypeStruct((96, 128), f32),
        in_specs=[pl.BlockSpec(memory_space=pltpu.SMEM)] + [any_spec] * 7,
        out_specs=pl.BlockSpec(memory_space=pltpu.VMEM),
        scratch_shapes=[
            pltpu.VMEM((K, N, rows, C), bf16),
            pltpu.VMEM((T, FFD), f32),
            pltpu.VMEM((T, FFD), f32),
            pltpu.VMEM((T, FFD), f32),
            pltpu.VMEM((T, 128), f32),
            pltpu.VMEM((T, 192), f32),
            pltpu.VMEM((WSLOTS, C, FFD), bf16),
            pltpu.VMEM((WSLOTS, C, FFD), bf16),
            pltpu.VMEM((WSLOTS, FFD, C), bf16),
            pltpu.VMEM(model_factor.shape, bf16),
            pltpu.VMEM(hidden_factor.shape[::-1], bf16),
            pltpu.VMEM((2, Y, Z, 96, 128), f32),
            pltpu.VMEM((Y, Z, 96, 128), f32),
            pltpu.VMEM((Z, 96, 128), WIRE),
            pltpu.VMEM((Z, 96, 128), WIRE),
            pltpu.VMEM((Z, 96, 128), WIRE),
            pltpu.VMEM((Z, 96, 128), WIRE),
            dma((K, N)),
            dma((K, 3 * Z + Z * Y + 3)),
            dma((K,)),
            dma((WSLOTS, 2)),
            dma((WSLOTS,)),
            dma((2,)),
            dma((2,)),
            dma((2,)),
            dma((Z,)),
            dma((Z,)),
        ],
        compiler_params=pltpu.CompilerParams(
            collective_id=0, has_side_effects=True, vmem_limit_bytes=60 * 1024 * 1024
        ),
        cost_estimate=pl.CostEstimate(
            flops=6 * T * D * FFD, bytes_accessed=6 * D * FFD, transcendentals=T * FFD
        ),
    )(lengths, tokens, cotangent, w_gate, w_up, w_down, model_factor, hidden_factor.T)
    first = out[0:64, 0:64].reshape(1, 4096)
    second = out[0:64, 64:128].reshape(1, 4096)
    third = jnp.concatenate([out[64:96, 0:64], out[64:96, 64:128]], axis=0).T.reshape(1, 4096)
    return jnp.concatenate([first, second, third], axis=1)


def solution(mesh):
    devices = mesh.shape["dp"]
    Y = 2 if mesh.shape["groups"] == 2 else 1
    placed = (
        P(("groups", "dp"), None),
        P(("groups", "dp"), None),
        P(None, "dp"),
        P(None, "dp"),
        P("dp", None),
        P(),
        P("dp", None),
        P("groups"),
    )
    return jax.shard_map(
        functools.partial(body, devices // (2 * Y), Y),
        mesh=mesh, in_specs=placed, out_specs=P(("groups", "dp"), None), check_vma=False,
    )
```

```python
import functools

import jax
import jax.numpy as jnp
from jax import lax
from jax.experimental import pallas as pl
from jax.experimental.pallas import tpu as pltpu
from jax.sharding import PartitionSpec as P

MESH = pl.DeviceIdType.MESH
PIECES = 5
WSLOTS = 2
Y_EVERY = 5
HOP = 1
AHEAD = 1
WIRE = jnp.bfloat16


def when(cond, fn):
    pl.when(cond)(fn)


def both(a, b):
    return jnp.logical_and(a, b)


def kernel(
    Z, Y, lengths, tokens, cot, w_gate, w_up, w_down, mf_hbm, hf_hbm, out,
    buf, acc_g, acc_u, acc_b, acc_m, feats, wg, wu, wd, mf, hf,
    part, r1, s2, r2, r3, s3,
    recv_sem, send_sem, own_sem, wsem, dsem, fsem, rs_send, rs_recv, z_send, z_recv,
):
    n, C = PIECES, wg.shape[1]
    K = 2 * n
    rows_dev = tokens.shape[0]
    N = Z * Y * 2
    T = N * rows_dev
    FFD = w_gate.shape[1]
    S = lengths.shape[0]
    me = lax.axis_index("dp")
    c = lax.rem(me, 2)
    y = lax.rem(me // 2, Y)
    z = me // (2 * Y)

    def index(zz, yy, cc):
        return (zz * Y + yy) * 2 + cc

    sib = index(z, y, 1 - c)
    ynb = index(z, Y - 1 - y, c)

    def column():
        for step in range(1, Z):
            yield step, lax.rem(z + step, Z)

    def own_copy(k_static):
        src = tokens if k_static < n else cot
        col = (k_static % n) * C
        return pltpu.make_async_copy(
            src.at[:, pl.ds(col, C)], buf.at[k_static, me], own_sem.at[k_static]
        )

    for k in range(K):
        own_copy(k).start()

    def weight_copies(k, slot):
        rows = pl.ds(pl.multiple_of(k * C, C), C)
        return (
            pltpu.make_async_copy(w_gate.at[rows, :], wg.at[slot], wsem.at[slot, 0]),
            pltpu.make_async_copy(w_up.at[rows, :], wu.at[slot], wsem.at[slot, 1]),
        )

    def down_copy(k, slot):
        cols = pl.ds(pl.multiple_of(k * C, C), C)
        return pltpu.make_async_copy(w_down.at[:, cols], wd.at[slot], dsem.at[slot])

    mf_copy = pltpu.make_async_copy(mf_hbm, mf, fsem.at[0])
    hf_copy = pltpu.make_async_copy(hf_hbm, hf, fsem.at[1])
    mf_copy.start()
    for j in range(WSLOTS):
        for cp in weight_copies(j, j):
            cp.start()
    hf_copy.start()
    for j in range(WSLOTS):
        down_copy(j, j).start()

    barrier = pltpu.get_barrier_semaphore()
    partners = [sib] + ([ynb] if Y > 1 else []) + [index(zz, y, c) for _, zz in column()]
    for p in partners:
        pl.semaphore_signal(barrier, inc=1, device_id={"dp": p}, device_id_type=MESH)
    pl.semaphore_wait(barrier, len(partners))

    def block(k, o, slot, dest):
        return pltpu.make_async_remote_copy(
            src_ref=buf.at[k, o],
            dst_ref=buf.at[k, o],
            send_sem=send_sem.at[k, slot],
            recv_sem=recv_sem.at[k, o],
            device_id={"dp": dest},
            device_id_type=MESH,
        )

    def wait_block(k, o):
        block(k, o, 0, sib).wait_recv()

    def y_first(k):
        return lax.rem(k, Y_EVERY) == Y_EVERY // 2

    def send_down(k, zz):
        return block(k, index(zz, y, c), zz, index(z - 1, y, c))

    def send_up(k, zz):
        return block(k, index(zz, y, c), zz, index(z + 1, y, c))

    def send_y(k, zz):
        return block(k, index(zz, y, c), Z + zz, ynb)

    def send_sib(k, zz, yy):
        return block(k, index(zz, yy, c), 2 * Z + zz * Y + yy, sib)

    def own_sends(k):
        yield z < Z - 1, lambda: block(k, me, 2 * Z + Z * Y, index(z + 1, y, c))
        yield z > 0, lambda: block(k, me, 2 * Z + Z * Y + 1, index(z - 1, y, c))
        if Y > 1:
            yield None, lambda: send_y(k, z)
        yield None, lambda: send_sib(k, z, y)

    def relay_sends(k, r, above):
        zz = z + r if above else z - r
        if above:
            yield z > 0, lambda: send_down(k, zz)
        else:
            yield z < Z - 1, lambda: send_up(k, zz)
        if Y > 1:
            yield jnp.logical_not(y_first(k)), lambda: send_y(k, zz)
        yield None, lambda: send_sib(k, zz, y)

    def other_sends(k, r, above):
        zz = z + r if above else z - r
        o = index(zz, Y - 1 - y, c)
        up, down = index(z + 1, y, c), index(z - 1, y, c)
        base = 2 * Z + Z * Y + 2
        if r == 0 or not above:
            yield both(y_first(k), z < Z - 1), lambda: block(k, o, base + zz, up)
        if r == 0:
            yield both(y_first(k), z > 0), lambda: block(k, o, base + Z, down)
        elif above:
            yield both(y_first(k), z > 0), lambda: block(k, o, base + zz, down)
        yield None, lambda: send_sib(k, zz, Y - 1 - y)

    def run(sends, act):
        for cond, make in sends:
            if cond is None:
                act(make())
            else:
                when(cond, functools.partial(lambda m: act(m()), make))

    start = lambda cp: cp.start()
    done = lambda cp: cp.wait_send()

    def here(r, above):
        return (z + r < Z) if above else (z - r >= 0)

    def own_stage(k):
        pltpu.make_async_copy(
            tokens.at[:, pl.ds(0, C)], buf.at[k, me], own_sem.at[k]
        ).wait()
        run(own_sends(k), start)

    def relay_stage(k, r):
        for above in (True, False):
            def arrived(above=above):
                zz = z + r if above else z - r
                wait_block(k, index(zz, y, c))
                run(relay_sends(k, r, above), start)
            when(here(r, above), arrived)

    def y_stage(k, r):
        for above in (True, False) if r else (True,):
            def arrived(above=above):
                zz = z + r if above else z - r
                wait_block(k, index(zz, Y - 1 - y, c))
                run(other_sends(k, r, above), start)
            when(here(r, above), arrived)

    def sib_stage(k):
        for zz in range(Z):
            for yy in range(Y):
                wait_block(k, index(zz, yy, 1 - c))

    for k in range(AHEAD):
        own_stage(k)

    acc_g[...] = jnp.zeros_like(acc_g)
    acc_u[...] = jnp.zeros_like(acc_u)
    acc_b[...] = jnp.zeros_like(acc_b)
    acc_m[...] = jnp.zeros_like(acc_m)
    mf_copy.wait()
    hf_copy.wait()
    lane = lax.broadcasted_iota(jnp.int32, (T, 128), 1)
    TILE = FFD
    GATING = 8 if n >= 8 else 4
    RB = T // GATING

    def project(rows):
        return lax.dot_general(
            rows, hf[...], (((1,), (1,)), ((), ())), preferred_element_type=jnp.float32
        )

    def compute(k):
        lhs = buf[k].reshape(T, C)
        kk = lax.rem(k, n)
        slot = lax.rem(kk, WSLOTS)
        mrows = pl.ds(pl.multiple_of(kk * C, C), C)
        mod = jnp.dot(lhs, mf[mrows, :], preferred_element_type=jnp.float32)
        first = k < n
        acc_m[...] += jnp.where((lane < 64) == first, mod, 0.0)

        def forward():
            for cp in weight_copies(kk, slot):
                cp.wait()

            def tile(j, carry):
                cols = pl.ds(pl.multiple_of(j * TILE, TILE), TILE)
                acc_g[:, cols] += jnp.dot(
                    lhs, wg[slot, :, cols], preferred_element_type=jnp.float32
                )
                acc_u[:, cols] += jnp.dot(
                    lhs, wu[slot, :, cols], preferred_element_type=jnp.float32
                )
                return carry

            lax.fori_loop(0, FFD // TILE, tile, 0)

            def more():
                for cp in weight_copies(kk + WSLOTS, slot):
                    cp.start()

            when(kk + WSLOTS < n, more)

        def backward():
            down_copy(kk, slot).wait()

            def tile(j, carry):
                cols = pl.ds(pl.multiple_of(j * TILE, TILE), TILE)
                acc_b[:, cols] += lax.dot_general(
                    lhs, wd[slot, cols, :], (((1,), (1,)), ((), ())),
                    preferred_element_type=jnp.float32,
                )
                return carry

            lax.fori_loop(0, FFD // TILE, tile, 0)
            when(kk + WSLOTS < n, lambda: down_copy(kk + WSLOTS, slot).start())

            def gating():
                rows = pl.ds(pl.multiple_of(kk * RB, RB), RB)
                gate = acc_g[rows, :]
                up = acc_u[rows, :]
                sig = jax.nn.sigmoid(gate)
                gs = gate * sig
                hidden = (gs * up).astype(jnp.bfloat16)
                acc_g[rows, :] = gs
                acc_u[rows, :] = up * sig * (1.0 + gate * (1.0 - sig))
                fh = project(hidden)
                feats[rows, 128:192] = fh[:, 128:192]

            when(kk < GATING, gating)

        when(first, forward)
        when(jnp.logical_not(first), backward)

    LAG = HOP * (Z + 1)

    def step(t, carry):
        for r in range(1, Z):
            k = t - HOP * r + HOP - 1
            when(both(k >= 0, k < K), functools.partial(relay_stage, k, r))
        if Y > 1:
            for r in range(Z):
                k = t - HOP * (r + 1) + HOP - 1
                when(both(k >= 0, k < K), functools.partial(y_stage, k, r))

        when(t + AHEAD < K, lambda: own_stage(t + AHEAD))

        def ready():
            sib_stage(t - LAG)
            compute(t - LAG)

        when(t >= LAG, ready)
        return carry

    lax.fori_loop(0, K + LAG, step, 0)

    FB = 128

    def finish(i, carry):
        rows = pl.ds(pl.multiple_of(i * FB, FB), FB)
        back = acc_b[rows, :]
        d_gate = (back * acc_u[rows, :]).astype(jnp.bfloat16)
        d_up = (back * acc_g[rows, :]).astype(jnp.bfloat16)
        fg = project(d_gate)
        fu = project(d_up)
        feats[rows, 0:128] = jnp.where(lane[:FB] < 64, fg[:, 0:128], fu[:, 0:128])
        return carry

    lax.fori_loop(0, T // FB, finish, 0)

    right = feats[...]
    right_hi = right.astype(jnp.bfloat16)
    right_lo = (right - right_hi.astype(jnp.float32)).astype(jnp.bfloat16)
    left = acc_m[...].T
    pos = lax.broadcasted_iota(jnp.int32, (128, T), 1)
    begin = jnp.int32(0)
    G = 4
    for s0 in range(0, S, G):
        his, los = [], []
        for s in range(s0, s0 + G):
            end = begin + lengths[s]
            picked = jnp.where(both(pos >= begin, pos < end), left, 0.0)
            hi = picked.astype(jnp.bfloat16)
            his.append(hi)
            los.append((picked - hi.astype(jnp.float32)).astype(jnp.bfloat16))
            begin = end
        hi = jnp.concatenate(his, axis=0)
        lo = jnp.concatenate(los, axis=0)
        sums = (
            jnp.dot(hi, right_hi, preferred_element_type=jnp.float32)
            + jnp.dot(hi, right_lo, preferred_element_type=jnp.float32)
            + jnp.dot(lo, right_hi, preferred_element_type=jnp.float32)
        )
        for s in range(s0, s0 + G):
            one = sums[(s - s0) * 128 : (s - s0 + 1) * 128]
            cc, yy, zz = s % 2, (s // 2) % Y, s // (2 * Y)
            part[cc, yy, zz, 0:64, :] = one[0:64, 0:128]
            part[cc, yy, zz, 64:96, :] = jnp.concatenate(
                [one[64:96, 128:192], one[96:128, 128:192]], axis=1
            )

    def drain(k, carry):
        run(own_sends(k), done)
        for r in range(1, Z):
            for above in (True, False):
                when(here(r, above), functools.partial(run, list(relay_sends(k, r, above)), done))
        if Y > 1:
            for r in range(Z):
                for above in (True, False) if r else (True,):
                    when(here(r, above), functools.partial(run, list(other_sends(k, r, above)), done))
        return carry

    core_send = pltpu.make_async_remote_copy(
        src_ref=part.at[1 - c], dst_ref=r1, send_sem=rs_send.at[0], recv_sem=rs_recv.at[0],
        device_id={"dp": sib}, device_id_type=MESH,
    )
    core_send.start()
    lax.fori_loop(0, n, drain, 0)
    core_send.wait_recv()
    if Y > 1:
        s2[...] = (part[c, 1 - y] + r1[1 - y]).astype(WIRE)
        y_send = pltpu.make_async_remote_copy(
            src_ref=s2, dst_ref=r2, send_sem=rs_send.at[1], recv_sem=rs_recv.at[1],
            device_id={"dp": ynb}, device_id_type=MESH,
        )
        y_send.start()
        lax.fori_loop(n, K, drain, 0)
        y_send.wait_recv()
    else:
        lax.fori_loop(n, K, drain, 0)

    def total(zz):
        value = part[c, y, zz] + r1[y, zz]
        if Y > 1:
            value = value + r2[zz].astype(jnp.float32)
        return value

    sends = []
    for step_z, zz in column():
        s3[step_z] = total(zz).astype(WIRE)
        cp = pltpu.make_async_remote_copy(
            src_ref=s3.at[step_z], dst_ref=r3.at[step_z], send_sem=z_send.at[step_z],
            recv_sem=z_recv.at[step_z], device_id={"dp": index(zz, y, c)}, device_id_type=MESH,
        )
        cp.start()
        sends.append(cp)
    value = total(z)
    for i, cp in enumerate(sends):
        cp.wait_recv()
        value = value + r3[i + 1].astype(jnp.float32)
    out[...] = value

    core_send.wait_send()
    if Y > 1:
        y_send.wait_send()
    for cp in sends:
        cp.wait_send()


def body(Z, Y, tokens, cotangent, w_gate, w_up, w_down, model_factor, hidden_factor, lengths):
    rows, D = tokens.shape
    FFD = w_gate.shape[1]
    N = Z * Y * 2
    T = N * rows
    n = PIECES
    C = D // n
    K = 2 * n
    f32, bf16 = jnp.float32, jnp.bfloat16
    any_spec = pl.BlockSpec(memory_space=pl.ANY)
    dma = pltpu.SemaphoreType.DMA
    out = pl.pallas_call(
        functools.partial(kernel, Z, Y),
        out_shape=jax.ShapeDtypeStruct((96, 128), f32),
        in_specs=[pl.BlockSpec(memory_space=pltpu.SMEM)] + [any_spec] * 7,
        out_specs=pl.BlockSpec(memory_space=pltpu.VMEM),
        scratch_shapes=[
            pltpu.VMEM((K, N, rows, C), bf16),
            pltpu.VMEM((T, FFD), f32),
            pltpu.VMEM((T, FFD), f32),
            pltpu.VMEM((T, FFD), f32),
            pltpu.VMEM((T, 128), f32),
            pltpu.VMEM((T, 192), f32),
            pltpu.VMEM((WSLOTS, C, FFD), bf16),
            pltpu.VMEM((WSLOTS, C, FFD), bf16),
            pltpu.VMEM((WSLOTS, FFD, C), bf16),
            pltpu.VMEM(model_factor.shape, bf16),
            pltpu.VMEM(hidden_factor.shape[::-1], bf16),
            pltpu.VMEM((2, Y, Z, 96, 128), f32),
            pltpu.VMEM((Y, Z, 96, 128), f32),
            pltpu.VMEM((Z, 96, 128), WIRE),
            pltpu.VMEM((Z, 96, 128), WIRE),
            pltpu.VMEM((Z, 96, 128), WIRE),
            pltpu.VMEM((Z, 96, 128), WIRE),
            dma((K, N)),
            dma((K, 3 * Z + Z * Y + 3)),
            dma((K,)),
            dma((WSLOTS, 2)),
            dma((WSLOTS,)),
            dma((2,)),
            dma((2,)),
            dma((2,)),
            dma((Z,)),
            dma((Z,)),
        ],
        compiler_params=pltpu.CompilerParams(
            collective_id=0, has_side_effects=True, vmem_limit_bytes=60 * 1024 * 1024
        ),
        cost_estimate=pl.CostEstimate(
            flops=6 * T * D * FFD, bytes_accessed=6 * D * FFD, transcendentals=T * FFD
        ),
    )(lengths, tokens, cotangent, w_gate, w_up, w_down, model_factor, hidden_factor.T)
    first = out[0:64, 0:64].reshape(1, 4096)
    second = out[0:64, 64:128].reshape(1, 4096)
    third = jnp.concatenate([out[64:96, 0:64], out[64:96, 64:128]], axis=0).T.reshape(1, 4096)
    return jnp.concatenate([first, second, third], axis=1)


def solution(mesh):
    devices = mesh.shape["dp"]
    Y = 2 if mesh.shape["groups"] == 2 else 1
    placed = (
        P(("groups", "dp"), None),
        P(("groups", "dp"), None),
        P(None, "dp"),
        P(None, "dp"),
        P("dp", None),
        P(),
        P("dp", None),
        P("groups"),
    )
    return jax.shard_map(
        functools.partial(body, devices // (2 * Y), Y),
        mesh=mesh, in_specs=placed, out_specs=P(("groups", "dp"), None), check_vma=False,
    )
```
